32 devices in a mesh: grp: 2 (over core), dev: 16 (over z, y, x).
Axes of the slice: x: 2, y: 2, z: 4, core: 2. Of those that a mesh axis runs over, the one named last changes fastest.
Arguments:
- centres: bfloat16 [65536, 512], P(('grp', 'dev')), may hold values from -12 to 12
- coefficients: float32 [100, 65536], P(None, ('grp', 'dev')), may hold values from -0.25 to 0.25
- targets: float32 [100, 512], P(None, ('grp', 'dev')), may hold values from -6 to 6
- batch_index: int32 [512], P(('grp', 'dev')), may hold values from 0 to 2047
- nys_index: int32 [512], P(('grp', 'dev')), may hold values from 0 to 2047
- eigvecs: float32 [512, 128], P(('grp', 'dev')), may hold values from -0.25 to 0.25
- eig_scale: float32 [128], replicated, may hold values from 0.1 to 2
Outputs:
- updated: float32 [100, 65536], P(None, ('grp', 'dev'))
- residual: float32 [100, 512], P(None, ('grp', 'dev'))
The draws below stay inside these ranges and needn't reach their ends.
Inputs may be any that keep to these rules, and one draw needn't show every extreme that they name: `batch_index`: entries of the k-th block of 16 name rows within the k-th block of 2048 centres. `nys_index`: entries of the k-th block of 16 name rows within the k-th block of 2048 centres.
All inputs are finite; a program needn't handle non-finite values.
Results may differ from the reference program's by a relative error of at most 0.0031.
Values may be sent and summed in bfloat16 or wider, within the bound.
A program may use at most 64 MiB of HBM per device.

```python
import math
import jax
import jax.numpy as jnp
from jax import lax

D = 512
O = 100
Q = 128
C_DEV = 2048
B_DEV = 16
S_DEV = 16
NC = 65536
BATCH = 512
SUB = 512
N_GRP = 2
N_DEV = 16


cluster_count = 16


def draw_centres(key, part):
    key_base = jax.random.fold_in(key, 11)
    key_scale = jax.random.fold_in(key, 12)
    key_means = jax.random.fold_in(key, 13)
    key_member = jax.random.fold_in(key, 14)
    member = jax.random.randint(key_member, (NC,), 0, cluster_count)
    means = 0.9 * jax.random.normal(key_means, (cluster_count, D), jnp.float32)
    noise = jnp.clip(jax.random.normal(key_base, (NC, D), jnp.float32), -4.0, 4.0)
    scales = jnp.exp(jax.random.uniform(key_scale, (NC, 1), jnp.float32, math.log(0.5), math.log(2.0)))
    rows = jnp.take(means, member, axis=0) + noise
    return jnp.clip(rows * scales, -12.0, 12.0).astype(jnp.bfloat16)


def set_ends(values, stream_key, smallest, largest):
    longest = values.shape.index(max(values.shape))
    spots = []
    for shift in (0, 1):
        where = [jax.random.randint(jax.random.fold_in(stream_key, axis), (), 0, length) for axis, length in enumerate(values.shape)]
        where[longest] = (where[longest] + shift) % values.shape[longest]
        spots.append(tuple(where))
    return values.at[spots[0]].set(smallest).at[spots[1]].set(largest)


def levels(rng, dims, cuts, smallest, largest):
    gain, own = 1.0, jax.random.fold_in(rng, 6)
    for position, parts in cuts:
        heights = jnp.exp(jax.random.uniform(jax.random.fold_in(own, position), (parts,), jnp.float32, smallest / len(cuts), largest / len(cuts)))
        gain = gain * jnp.repeat(heights, dims[position] // parts).reshape([-1 if axis == position else 1 for axis in range(len(dims))])
    return gain


def normal_values(key, shape, width, reach, cuts=(), kind=jnp.bfloat16):
    factor_of = levels(key, shape, cuts, -0.22, 0.18) if cuts else 1.0
    entries = jax.random.normal(key, shape, jnp.float32) * width * factor_of
    return jnp.minimum(jnp.maximum(entries, -reach), reach).astype(kind)


def setup_inputs(seed: int = 0) -> dict:
    key_list = jax.random.split(jax.random.key(seed), 8)
    centres = draw_centres(jax.random.fold_in(key_list[7], 71), 0)
    coefficients = normal_values(key_list[1], (O, NC), (NC // 100) ** -0.5, 0.25, ((1, 32),), jnp.float32)
    targets = normal_values(key_list[2], (O, BATCH), 1.0, 6.0, ((1, 32),), jnp.float32)
    batch_index = set_ends(jax.random.randint(key_list[3], (BATCH,), 0, C_DEV), jax.random.fold_in(key_list[3], 1), 0, C_DEV - 1).astype(jnp.int32)
    nys_index = set_ends(jax.random.randint(key_list[4], (SUB,), 0, C_DEV), jax.random.fold_in(key_list[4], 1), 0, C_DEV - 1).astype(jnp.int32)
    eigvecs = normal_values(key_list[5], (SUB, Q), SUB ** -0.5, 0.25, ((0, 32),), jnp.float32)
    eig_scale = jnp.clip(jnp.exp(jax.random.uniform(key_list[6], (Q,), jnp.float32, math.log(0.1), math.log(2.0))), 0.1, 2.0)
    return dict(centres=centres, coefficients=coefficients, targets=targets, batch_index=batch_index, nys_index=nys_index, eigvecs=eigvecs, eig_scale=eig_scale)


step_rate = 1.0

def kernel_block(left_rows, right_rows, spread):
    left_sq = lax.optimization_barrier(jnp.sum(jnp.square(left_rows.astype(jnp.float32)), axis=1))
    right_sq = lax.optimization_barrier(jnp.sum(jnp.square(right_rows.astype(jnp.float32)), axis=1))
    cross_dot = lax.dot_general(left_rows, right_rows, (((1,), (1,)), ((), ())), preferred_element_type=jnp.float32)
    distance = jnp.sqrt(jnp.maximum(left_sq[:, None] + right_sq[None, :] - 2.0 * cross_dot, 1.0))
    return jnp.exp(-distance / spread)

def reference(centres, coefficients, targets, batch_index, nys_index, eigvecs, eig_scale):
    spread = 0.7 * math.sqrt(D)
    shards = N_GRP * N_DEV
    batch_global = jnp.arange(BATCH, dtype=jnp.int32) // B_DEV * C_DEV + batch_index.astype(jnp.int32)
    nys_global = jnp.arange(SUB, dtype=jnp.int32) // S_DEV * C_DEV + nys_index.astype(jnp.int32)
    batch_rows = centres[batch_global]
    nys_rows = centres[nys_global]
    coef_bf = coefficients.astype(jnp.bfloat16)
    centre_blocks = centres.reshape(shards, C_DEV, D)
    coef_blocks = jnp.transpose(coef_bf.reshape(O, shards, C_DEV), (1, 0, 2))

    def add_shard(running, block_pair):
        centre_block, coef_block = block_pair
        kernel = kernel_block(batch_rows, centre_block, spread).astype(jnp.bfloat16)
        partial_value = lax.dot_general(coef_block, kernel, (((1,), (1,)), ((), ())), preferred_element_type=jnp.float32)
        return (running + partial_value, None)
    predicted, _ = lax.scan(add_shard, jnp.zeros((O, BATCH), jnp.float32), (centre_blocks, coef_blocks))
    residual = predicted - targets
    nys_kernel = kernel_block(nys_rows, batch_rows, spread)
    nys_sums = lax.dot_general(nys_kernel, residual, (((1,), (1,)), ((), ())), precision=lax.Precision.HIGHEST)
    projected = lax.dot_general(eigvecs, nys_sums, (((0,), (0,)), ((), ())), precision=lax.Precision.HIGHEST)
    correction = jnp.dot(eigvecs, eig_scale[:, None] * projected, precision=lax.Precision.HIGHEST)
    updated = coefficients.at[:, batch_global].add(-step_rate * residual)
    updated = updated.at[:, nys_global].add(step_rate * jnp.transpose(correction))
    return (updated, residual)
```

```python
import functools
import math

import jax
import jax.numpy as jnp
from jax import lax
from jax.experimental import pallas as pl
from jax.experimental.pallas import tpu as pltpu
from jax.sharding import PartitionSpec as P

MESH = pl.DeviceIdType.MESH
HIGHEST = lax.Precision.HIGHEST
NN = (((1,), (0,)), ((), ()))
NT = (((1,), (1,)), ((), ()))
TN = (((0,), (0,)), ((), ()))


def mm(a, b, dims=NN, precision=None):
    return lax.dot_general(a, b, dims, precision=precision, preferred_element_type=jnp.float32)


def split_square(x):
    f = x.astype(jnp.float32)
    f = f * f
    high = f.astype(jnp.bfloat16)
    low = (f - high.astype(jnp.float32)).astype(jnp.bfloat16)
    return high, low


def square_column(x):
    high, low = split_square(x)
    ones = jnp.ones((x.shape[1], 128), jnp.bfloat16)
    return mm(high, ones) + mm(low, ones)


def square_row(x):
    high, low = split_square(x)
    ones = jnp.ones((8, x.shape[1]), jnp.bfloat16)
    return (mm(ones, high, NT) + mm(ones, low, NT))[0:1]


def laplace(left, left_sq, minus_two_right, right_sq, rate):
    cross = mm(left, minus_two_right, NT)
    wide = jnp.concatenate([left_sq] * (cross.shape[1] // 128), axis=1)
    d2 = jnp.maximum((wide + right_sq) + cross, 1.0)
    return jnp.exp2((d2 * lax.rsqrt(d2)) * rate)


def kernel(n_grp, n_dev, bidx, nidx, scale, targets, eig, centres_hbm, coef_hbm,
           updated, res_out,
           centres, coef, coef_bf, csq, rows, nys, eigs, pick, acc, part, got, res, gain, square,
           local_sem, send_sem, recv_sem):
    n = n_grp * n_dev
    grp, dev = lax.axis_index("grp"), lax.axis_index("dev")
    me = grp * n_dev + dev
    c_dev, feat = centres.shape
    outs = coef.shape[0]
    b_dev, s_dev = bidx.shape[0], nidx.shape[0]
    batch, sub = rows.shape[0], nys.shape[0]
    rate = -1.0 / (0.7 * math.sqrt(feat) * math.log(2.0))
    wide_out = part.shape[1]

    load_centres = pltpu.make_async_copy(centres_hbm, centres, local_sem.at[0])
    load_coef = pltpu.make_async_copy(coef_hbm, coef, local_sem.at[1])
    load_centres.start()
    load_coef.start()

    def peer_id(k):
        p = lax.rem(me + k, n)
        return p, {"grp": p // n_dev, "dev": lax.rem(p, n_dev)}

    barrier = pltpu.get_barrier_semaphore()

    @pl.loop(1, n)
    def _(k):
        _, where = peer_id(k)
        pl.semaphore_signal(barrier, inc=1, device_id=where, device_id_type=MESH)

    def block(ref, p, size):
        return ref.at[pl.ds(pl.multiple_of(p * size, size), size)]

    def send_all(src, dst, size, slot, gather):
        @pl.loop(1, n)
        def _(k):
            p, where = peer_id(k)
            pltpu.make_async_remote_copy(
                src_ref=block(src, me if gather else p, size), dst_ref=block(dst, me, size),
                send_sem=send_sem.at[slot], recv_sem=recv_sem.at[slot],
                device_id=where, device_id_type=MESH).start()

    def all_but_one(ref, size, slot):
        piece = ref.at[pl.ds(0, (n - 1) * size)]
        _, where = peer_id(1)
        return pltpu.make_async_remote_copy(
            src_ref=piece, dst_ref=piece, send_sem=send_sem.at[slot], recv_sem=recv_sem.at[slot],
            device_id=where, device_id_type=MESH)

    total = b_dev + s_dev
    spot = lax.broadcasted_iota(jnp.int32, (total, 128), 0)
    index = jnp.zeros((total, 128), jnp.int32)
    for r in range(b_dev):
        index = jnp.where(spot == r, bidx[r], index)
    for r in range(s_dev):
        index = jnp.where(spot == b_dev + r, nidx[r], index)
    index = jnp.concatenate([index] * (c_dev // 128), axis=1)
    hit = lax.broadcasted_iota(jnp.int32, (total, c_dev), 1) == index
    pick[...] = jnp.where(hit, 1.0, 0.0).astype(jnp.bfloat16)

    load_centres.wait()
    own = mm(pick[...], centres[...]).astype(jnp.bfloat16)
    block(rows, me, b_dev)[...] = own[:b_dev]
    block(nys, me, s_dev)[...] = own[b_dev:]
    block(eigs, me, s_dev)[...] = eig[...]

    pl.semaphore_wait(barrier, n - 1)
    send_all(rows, rows, b_dev, 0, True)
    send_all(nys, nys, s_dev, 1, True)
    send_all(eigs, eigs, s_dev, 2, True)

    step = 256 if c_dev % 256 == 0 else 128

    @pl.loop(0, c_dev // step)
    def _(i):
        piece = pl.ds(pl.multiple_of(i * step, step), step)
        csq[piece, :] = square_column(centres[piece, :])

    load_coef.wait()
    coef_bf[...] = coef[...].astype(jnp.bfloat16)
    square[...] = jnp.zeros_like(square)
    square[0:outs, 0:b_dev] = targets[...]
    target = jnp.transpose(square[...])[0:b_dev]
    acc[...] = jnp.zeros_like(acc)

    width = acc.shape[1]
    all_but_one(rows, b_dev, 0).wait_recv()

    @pl.loop(0, batch // width)
    def _(j):
        across = pl.ds(pl.multiple_of(j * width, width), width)
        piece_rows = rows[across, :]
        bsq = square_row(piece_rows)
        minus_two = piece_rows * jnp.bfloat16(-2.0)
        sums = jnp.zeros((outs, width), jnp.float32)
        for i in range(c_dev // step):
            down = slice(i * step, (i + 1) * step)
            k = laplace(centres[down, :], csq[down, :], minus_two, bsq, rate).astype(jnp.bfloat16)
            sums = sums + mm(coef_bf[:, down], k)
        acc[0:outs, :] = sums
        part[across, :] = jnp.transpose(acc[...])

    send_all(part, got, b_dev, 3, False)
    block(got, me, b_dev)[...] = block(part, me, b_dev)[...]

    all_but_one(nys, s_dev, 1).wait_recv()
    all_but_one(eigs, s_dev, 2).wait_recv()
    weights = mm(eig[...] * scale[...], eigs[...], NT, HIGHEST)
    tall = min(512, sub)

    @pl.loop(0, batch // width)
    def _(j):
        across = pl.ds(pl.multiple_of(j * width, width), width)
        piece_rows = rows[across, :]
        bsq = square_row(piece_rows)
        minus_two = piece_rows * jnp.bfloat16(-2.0)
        total_gain = jnp.zeros((s_dev, width), jnp.float32)
        for i in range(sub // tall):
            piece_nys = nys[i * tall:(i + 1) * tall, :]
            kn = laplace(piece_nys, square_column(piece_nys), minus_two, bsq, rate)
            total_gain = total_gain + mm(weights[:, i * tall:(i + 1) * tall], kn, NN, HIGHEST)
        gain[:, across] = total_gain

    all_but_one(got, b_dev, 3).wait_recv()
    own_res = jnp.sum(got[...].reshape(n, b_dev, wide_out), axis=0) - target
    block(res, me, b_dev)[...] = own_res
    send_all(res, res, b_dev, 4, True)
    square[0:b_dev, :] = own_res
    res_out[...] = jnp.transpose(square[...])[0:outs, 0:b_dev]

    all_but_one(res, b_dev, 4).wait_recv()
    correction = mm(gain[...], res[...], NN, HIGHEST)
    change = jnp.concatenate([-own_res, correction], axis=0)
    high = change.astype(jnp.bfloat16)
    rest = change - high.astype(jnp.float32)
    middle = rest.astype(jnp.bfloat16)
    low = (rest - middle.astype(jnp.float32)).astype(jnp.bfloat16)
    change3 = jnp.concatenate([high, middle, low], axis=0)
    pick3 = jnp.concatenate([pick[...]] * 3, axis=0)
    updated[...] = coef[...] + mm(change3, pick3, TN)[0:outs]

    for slot, ref, size in ((0, rows, b_dev), (1, nys, s_dev), (2, eigs, s_dev),
                            (3, part, b_dev), (4, res, b_dev)):
        all_but_one(ref, size, slot).wait_send()


def per_device(n_grp, n_dev, centres, coefficients, targets, batch_index, nys_index, eigvecs, eig_scale):
    n = n_grp * n_dev
    c_dev, feat = centres.shape
    outs = coefficients.shape[0]
    b_dev, s_dev, q = batch_index.shape[0], nys_index.shape[0], eigvecs.shape[1]
    batch, sub = n * b_dev, n * s_dev
    wide_out = -(-outs // 128) * 128
    width = min(512, batch)
    vmem = pl.BlockSpec(memory_space=pltpu.VMEM)
    smem = pl.BlockSpec(memory_space=pltpu.SMEM)
    hbm = pl.BlockSpec(memory_space=pl.ANY)
    f32, bf16 = jnp.float32, jnp.bfloat16
    updated, residual = pl.pallas_call(
        functools.partial(kernel, n_grp, n_dev),
        out_shape=(jax.ShapeDtypeStruct((outs, c_dev), f32), jax.ShapeDtypeStruct((outs, b_dev), f32)),
        in_specs=[smem, smem, vmem, vmem, vmem, hbm, hbm],
        out_specs=(vmem, vmem),
        scratch_shapes=[
            pltpu.VMEM((c_dev, feat), bf16),
            pltpu.VMEM((outs, c_dev), f32),
            pltpu.VMEM((outs, c_dev), bf16),
            pltpu.VMEM((c_dev, 128), f32),
            pltpu.VMEM((batch, feat), bf16),
            pltpu.VMEM((sub, feat), bf16),
            pltpu.VMEM((sub, q), f32),
            pltpu.VMEM((b_dev + s_dev, c_dev), bf16),
            pltpu.VMEM((wide_out, width), f32),
            pltpu.VMEM((batch, wide_out), f32),
            pltpu.VMEM((batch, wide_out), f32),
            pltpu.VMEM((batch, wide_out), f32),
            pltpu.VMEM((s_dev, batch), f32),
            pltpu.VMEM((wide_out, wide_out), f32),
            pltpu.SemaphoreType.DMA((2,)),
            pltpu.SemaphoreType.DMA((5,)),
            pltpu.SemaphoreType.DMA((5,)),
        ],
        compiler_params=pltpu.CompilerParams(
            collective_id=0, has_side_effects=True, vmem_limit_bytes=56 * 1024 * 1024),
    )(batch_index, nys_index, eig_scale.reshape(1, q), targets, eigvecs, centres, coefficients)
    return updated, residual


def solution(mesh):
    both = ("grp", "dev")
    in_specs = (P(both, None), P(None, both), P(None, both), P(both), P(both), P(both, None), P())
    out_specs = (P(None, both), P(None, both))
    return jax.shard_map(
        functools.partial(per_device, mesh.shape["grp"], mesh.shape["dev"]),
        mesh=mesh, in_specs=in_specs, out_specs=out_specs, check_vma=False)
```

```python
import functools
import math

import jax
import jax.numpy as jnp
from jax import lax
from jax.experimental import pallas as pl
from jax.experimental.pallas import tpu as pltpu
from jax.sharding import PartitionSpec as P

MESH = pl.DeviceIdType.MESH
HIGHEST = lax.Precision.HIGHEST
NN = (((1,), (0,)), ((), ()))
NT = (((1,), (1,)), ((), ()))
TN = (((0,), (0,)), ((), ()))


def mm(a, b, dims=NN, precision=None):
    return lax.dot_general(a, b, dims, precision=precision, preferred_element_type=jnp.float32)


def split_square(x):
    f = x.astype(jnp.float32)
    f = f * f
    high = f.astype(jnp.bfloat16)
    low = (f - high.astype(jnp.float32)).astype(jnp.bfloat16)
    return high, low


def square_column(x):
    high, low = split_square(x)
    ones = jnp.ones((x.shape[1], 128), jnp.bfloat16)
    return mm(high, ones) + mm(low, ones)


def square_row(x):
    high, low = split_square(x)
    ones = jnp.ones((8, x.shape[1]), jnp.bfloat16)
    return (mm(ones, high, NT) + mm(ones, low, NT))[0:1]


def laplace(left, left_sq, minus_two_right, right_sq, rate):
    cross = mm(left, minus_two_right, NT)
    wide = jnp.concatenate([left_sq] * (cross.shape[1] // 128), axis=1)
    d2 = jnp.maximum((wide + right_sq) + cross, 1.0)
    return jnp.exp2((d2 * lax.rsqrt(d2)) * rate)


def one_hot(bidx, nidx, c_dev, first):
    b_dev, s_dev = bidx.shape[0], nidx.shape[0]
    total = b_dev + s_dev
    spot = lax.broadcasted_iota(jnp.int32, (total, 128), 0)
    index = jnp.zeros((total, 128), jnp.int32)
    for r in range(b_dev):
        index = jnp.where(spot == r, bidx[r], index)
    for r in range(s_dev):
        index = jnp.where(spot == b_dev + r, nidx[r], index)
    index = jnp.concatenate([index - first] * (c_dev // 128), axis=1)
    hit = lax.broadcasted_iota(jnp.int32, (total, c_dev), 1) == index
    return jnp.where(hit, 1.0, 0.0).astype(jnp.bfloat16)


def kernel(n_grp, n_dev, bidx, nidx, scale, targets, eig, centres_hbm, coef_hbm,
           change,
           centres, coef, coef_bf, csq, rows, nys, eigs, acc, part, pair, summed, got, res, gain, target,
           local_sem, send_sem, recv_sem, pass_send, pass_recv, pair_send, pair_recv, sum_send, sum_recv):
    n = n_grp * n_dev
    grp, dev = lax.axis_index("grp"), lax.axis_index("dev")
    me = grp * n_dev + dev
    c_dev, feat = centres.shape
    outs = coef.shape[0]
    b_dev, s_dev = bidx.shape[0], nidx.shape[0]
    batch, sub = rows.shape[0], nys.shape[0]
    rate = -1.0 / (0.7 * math.sqrt(feat) * math.log(2.0))
    wide_out = part.shape[1]
    band = n_dev * b_dev

    load_centres = pltpu.make_async_copy(centres_hbm, centres, local_sem.at[0])
    load_coef = pltpu.make_async_copy(coef_hbm, coef, local_sem.at[1])
    load_centres.start()
    load_coef.start()

    def chip(k):
        p = lax.rem(dev + k, n_dev)
        return p, {"grp": grp, "dev": p}

    def core(k):
        p = lax.rem(grp + k, n_grp)
        return p, {"grp": p, "dev": dev}

    barrier = pltpu.get_barrier_semaphore()

    @pl.loop(1, n_dev)
    def _(k):
        pl.semaphore_signal(barrier, inc=1, device_id=chip(k)[1], device_id_type=MESH)

    for k in range(1, n_grp):
        pl.semaphore_signal(barrier, inc=1, device_id=core(k)[1], device_id_type=MESH)

    def block(ref, p, size):
        return ref.at[pl.ds(pl.multiple_of(p * size, size), size)]

    def chip_copy(ref, size, slot, k):
        mine = block(ref, me, size)
        return pltpu.make_async_remote_copy(
            src_ref=mine, dst_ref=mine, send_sem=send_sem.at[slot], recv_sem=recv_sem.at[slot, k],
            device_id=chip(k)[1], device_id_type=MESH)

    def pass_on(ref, size, slot, source):
        piece = block(ref, grp * n_dev + source, size)
        for k in range(1, n_grp):
            pltpu.make_async_remote_copy(
                src_ref=piece, dst_ref=piece, send_sem=pass_send.at[slot], recv_sem=pass_recv.at[slot],
                device_id=core(k)[1], device_id_type=MESH).start()

    def gather_start(ref, size, slot):
        @pl.loop(1, n_dev)
        def _(k):
            chip_copy(ref, size, slot, k).start()

        pass_on(ref, size, slot, dev)

    def gather_pass(ref, size, slot):
        @pl.loop(1, n_dev)
        def _(k):
            chip_copy(ref, size, slot, k).wait_recv()
            pass_on(ref, size, slot, lax.rem(dev + n_dev - k, n_dev))

    def many(ref, count, send, recv, where):
        piece = ref.at[pl.ds(0, count)]
        return pltpu.make_async_remote_copy(
            src_ref=piece, dst_ref=piece, send_sem=send, recv_sem=recv, device_id=where, device_id_type=MESH)

    def passed(ref, size, slot):
        return many(ref, (n_grp - 1) * n_dev * size, pass_send.at[slot], pass_recv.at[slot], core(1)[1])

    def gather_sent(ref, size, slot):
        many(ref, (n_dev - 1) * size, send_sem.at[slot], recv_sem.at[slot, 0], chip(1)[1]).wait_send()
        passed(ref, size, slot).wait_send()

    pick = one_hot(bidx, nidx, c_dev, 0)
    block(eigs, me, s_dev)[...] = eig[...]
    pl.semaphore_wait(barrier, (n_dev - 1) + (n_grp - 1))
    gather_start(eigs, s_dev, 2)

    load_centres.wait()
    own = mm(pick, centres[...]).astype(jnp.bfloat16)
    block(rows, me, b_dev)[...] = own[:b_dev]
    block(nys, me, s_dev)[...] = own[b_dev:]
    gather_start(rows, b_dev, 0)
    gather_start(nys, s_dev, 1)

    step = 256 if c_dev % 256 == 0 else 128

    @pl.loop(0, c_dev // step)
    def _(i):
        piece = pl.ds(pl.multiple_of(i * step, step), step)
        csq[piece, :] = square_column(centres[piece, :])

    load_coef.wait()
    coef_bf[...] = coef[...].astype(jnp.bfloat16)
    target[...] = jnp.zeros_like(target)
    target[:, 0:outs] = targets[...]
    acc[...] = jnp.zeros_like(acc)

    width = acc.shape[1]
    gather_pass(rows, b_dev, 0)

    per_band = band // width

    @pl.loop(0, n_grp * per_band)
    def _(j):
        @pl.when(j == per_band)
        def _():
            passed(rows, b_dev, 0).wait_recv()

        first = lax.rem(grp + j // per_band, n_grp) * band + lax.rem(j, per_band) * width
        across = pl.ds(pl.multiple_of(first, width), width)
        piece_rows = rows[across, :]
        bsq = square_row(piece_rows)
        minus_two = piece_rows * jnp.bfloat16(-2.0)
        sums = jnp.zeros((outs, width), jnp.float32)
        for i in range(c_dev // step):
            down = slice(i * step, (i + 1) * step)
            k = laplace(centres[down, :], csq[down, :], minus_two, bsq, rate).astype(jnp.bfloat16)
            sums = sums + mm(coef_bf[:, down], k)
        acc[0:outs, :] = sums
        part[across, :] = jnp.transpose(acc[...])

    for k in range(1, n_grp):
        g, where = core(k)
        pltpu.make_async_remote_copy(
            src_ref=block(part, g, band), dst_ref=pair.at[pl.ds((k - 1) * band, band)],
            send_sem=pair_send, recv_sem=pair_recv, device_id=where, device_id_type=MESH).start()
    pairs = many(pair, (n_grp - 1) * band, pair_send, pair_recv, core(1)[1])
    pairs.wait_recv()
    both = block(part, grp, band)[...]
    for k in range(1, n_grp):
        both = both + pair[(k - 1) * band:k * band, :]
    summed[...] = both

    @pl.loop(1, n_dev)
    def _(k):
        p, where = chip(k)
        pltpu.make_async_remote_copy(
            src_ref=block(summed, p, b_dev), dst_ref=block(got, dev, b_dev),
            send_sem=sum_send, recv_sem=sum_recv, device_id=where, device_id_type=MESH).start()

    block(got, dev, b_dev)[...] = block(summed, dev, b_dev)[...]

    gather_pass(eigs, s_dev, 2)
    gather_pass(nys, s_dev, 1)
    sums_in = many(got, (n_dev - 1) * b_dev, sum_send, sum_recv, chip(1)[1])

    def make_gain():
        passed(eigs, s_dev, 2).wait_recv()
        passed(nys, s_dev, 1).wait_recv()
        weights = mm(eig[...] * scale[...], eigs[...], NT, HIGHEST)
        tall = min(512, sub)
        span = min(512, batch)

        @pl.loop(0, batch // span)
        def _(j):
            across = pl.ds(pl.multiple_of(j * span, span), span)
            piece_rows = rows[across, :]
            bsq = square_row(piece_rows)
            minus_two = piece_rows * jnp.bfloat16(-2.0)
            total_gain = jnp.zeros((s_dev, span), jnp.float32)
            for i in range(sub // tall):
                piece_nys = nys[i * tall:(i + 1) * tall, :]
                kn = laplace(piece_nys, square_column(piece_nys), minus_two, bsq, rate)
                total_gain = total_gain + mm(weights[:, i * tall:(i + 1) * tall], kn, NN, HIGHEST)
            gain[:, across] = total_gain

    sums_in.wait_recv()
    own_res = jnp.sum(got[...].reshape(n_dev, b_dev, wide_out), axis=0) - target[...]
    block(res, me, b_dev)[...] = own_res
    gather_start(res, b_dev, 3)
    change[0:b_dev, :] = own_res
    make_gain()
    gather_pass(res, b_dev, 3)
    passed(res, b_dev, 3).wait_recv()
    change[b_dev:, :] = mm(gain[...], res[...], NN, HIGHEST)

    for slot, ref, size in ((0, rows, b_dev), (1, nys, s_dev), (2, eigs, s_dev), (3, res, b_dev)):
        gather_sent(ref, size, slot)
    pairs.wait_send()
    sums_in.wait_send()


def update_kernel(bidx, nidx, change, coef, updated, res_out):
    outs, width = coef.shape
    b_dev = bidx.shape[0]
    pick = one_hot(bidx, nidx, width, pl.program_id(0) * width)
    own_res = change[0:b_dev, :]
    both = jnp.concatenate([-own_res, change[b_dev:, :]], axis=0)
    high = both.astype(jnp.bfloat16)
    rest = both - high.astype(jnp.float32)
    middle = rest.astype(jnp.bfloat16)
    low = (rest - middle.astype(jnp.float32)).astype(jnp.bfloat16)
    both3 = jnp.concatenate([high, middle, low], axis=0)
    pick3 = jnp.concatenate([pick] * 3, axis=0)
    updated[...] = coef[...] + mm(both3, pick3, TN)[0:outs]
    res_out[...] = own_res[:, 0:outs]


def per_device(n_grp, n_dev, centres, coefficients, targets, batch_index, nys_index, eigvecs, eig_scale):
    n = n_grp * n_dev
    c_dev, feat = centres.shape
    outs = coefficients.shape[0]
    b_dev, s_dev, q = batch_index.shape[0], nys_index.shape[0], eigvecs.shape[1]
    batch, sub, band = n * b_dev, n * s_dev, n_dev * b_dev
    wide_out = -(-outs // 128) * 128
    width = min(512, band)
    vmem = pl.BlockSpec(memory_space=pltpu.VMEM)
    smem = pl.BlockSpec(memory_space=pltpu.SMEM)
    hbm = pl.BlockSpec(memory_space=pl.ANY)
    f32, bf16, dma = jnp.float32, jnp.bfloat16, pltpu.SemaphoreType.DMA
    change = pl.pallas_call(
        functools.partial(kernel, n_grp, n_dev),
        out_shape=jax.ShapeDtypeStruct((b_dev + s_dev, wide_out), f32),
        in_specs=[smem, smem, vmem, vmem, vmem, hbm, hbm],
        out_specs=vmem,
        scratch_shapes=[
            pltpu.VMEM((c_dev, feat), bf16),
            pltpu.VMEM((outs, c_dev), f32),
            pltpu.VMEM((outs, c_dev), bf16),
            pltpu.VMEM((c_dev, 128), f32),
            pltpu.VMEM((batch, feat), bf16),
            pltpu.VMEM((sub, feat), bf16),
            pltpu.VMEM((sub, q), f32),
            pltpu.VMEM((wide_out, width), f32),
            pltpu.VMEM((batch, wide_out), f32),
            pltpu.VMEM(((n_grp - 1) * band, wide_out), f32),
            pltpu.VMEM((band, wide_out), f32),
            pltpu.VMEM((band, wide_out), f32),
            pltpu.VMEM((batch, wide_out), f32),
            pltpu.VMEM((s_dev, batch), f32),
            pltpu.VMEM((b_dev, wide_out), f32),
            dma((2,)), dma((4,)), dma((4, n_dev)), dma((4,)), dma((4,)), dma, dma, dma, dma,
        ],
        compiler_params=pltpu.CompilerParams(
            collective_id=0, has_side_effects=True, vmem_limit_bytes=56 * 1024 * 1024),
    )(batch_index, nys_index, eig_scale.reshape(1, q), targets.T, eigvecs, centres, coefficients)
    columns = 1024 if c_dev % 1024 == 0 else c_dev
    whole = pl.BlockSpec((b_dev + s_dev, wide_out), lambda i: (0, 0))
    tile = pl.BlockSpec((outs, columns), lambda i: (0, i))
    updated, residual = pl.pallas_call(
        update_kernel,
        grid=(c_dev // columns,),
        out_shape=(jax.ShapeDtypeStruct((outs, c_dev), f32), jax.ShapeDtypeStruct((b_dev, outs), f32)),
        in_specs=[smem, smem, whole, tile],
        out_specs=(tile, pl.BlockSpec((b_dev, outs), lambda i: (0, 0))),
    )(batch_index, nys_index, change, coefficients)
    return updated, residual.T


def solution(mesh):
    both = ("grp", "dev")
    in_specs = (P(both, None), P(None, both), P(None, both), P(both), P(both), P(both, None), P())
    out_specs = (P(None, both), P(None, both))
    return jax.shard_map(
        functools.partial(per_device, mesh.shape["grp"], mesh.shape["dev"]),
        mesh=mesh, in_specs=in_specs, out_specs=out_specs, check_vma=False)
```

```python
import functools
import math

import jax
import jax.numpy as jnp
from jax import lax
from jax.experimental import pallas as pl
from jax.experimental.pallas import tpu as pltpu
from jax.sharding import PartitionSpec as P

MESH = pl.DeviceIdType.MESH
HIGHEST = lax.Precision.HIGHEST
NN = (((1,), (0,)), ((), ()))
NT = (((1,), (1,)), ((), ()))
TN = (((0,), (0,)), ((), ()))


def mm(a, b, dims=NN, precision=None):
    return lax.dot_general(a, b, dims, precision=precision, preferred_element_type=jnp.float32)


def split_square(x):
    f = x.astype(jnp.float32)
    f = f * f
    high = f.astype(jnp.bfloat16)
    low = (f - high.astype(jnp.float32)).astype(jnp.bfloat16)
    return high, low


def square_column(x):
    high, low = split_square(x)
    ones = jnp.ones((x.shape[1], 128), jnp.bfloat16)
    return mm(high, ones) + mm(low, ones)


def square_row(x):
    high, low = split_square(x)
    ones = jnp.ones((8, x.shape[1]), jnp.bfloat16)
    return (mm(ones, high, NT) + mm(ones, low, NT))[0:1]


def laplace(left, left_sq, minus_two_right, right_sq, rate):
    cross = mm(left, minus_two_right, NT)
    wide = jnp.concatenate([left_sq] * (cross.shape[1] // 128), axis=1)
    d2 = jnp.maximum((wide + right_sq) + cross, 1.0)
    return jnp.exp2((d2 * lax.rsqrt(d2)) * rate)


def one_hot(bidx, nidx, c_dev, first):
    b_dev, s_dev = bidx.shape[0], nidx.shape[0]
    total = b_dev + s_dev
    spot = lax.broadcasted_iota(jnp.int32, (total, 128), 0)
    index = jnp.zeros((total, 128), jnp.int32)
    for r in range(b_dev):
        index = jnp.where(spot == r, bidx[r], index)
    for r in range(s_dev):
        index = jnp.where(spot == b_dev + r, nidx[r], index)
    index = jnp.concatenate([index - first] * (c_dev // 128), axis=1)
    hit = lax.broadcasted_iota(jnp.int32, (total, c_dev), 1) == index
    return jnp.where(hit, 1.0, 0.0).astype(jnp.bfloat16)


def kernel(n_grp, n_dev, bidx, nidx, scale, targets, eig, centres_hbm, coef_hbm,
           change,
           centres, coef, coef_bf, csq, rows, nys, eigs, acc, part, pair, summed, got, res, gain, target,
           local_sem, send_sem, recv_sem, pass_send, pass_recv, pair_send, pair_recv, sum_send, sum_recv):
    n = n_grp * n_dev
    grp, dev = lax.axis_index("grp"), lax.axis_index("dev")
    me = grp * n_dev + dev
    c_dev, feat = centres.shape
    outs = coef.shape[0]
    b_dev, s_dev = bidx.shape[0], nidx.shape[0]
    batch, sub = rows.shape[0], nys.shape[0]
    rate = -1.0 / (0.7 * math.sqrt(feat) * math.log(2.0))
    wide_out = part.shape[1]
    band = n_dev * b_dev

    load_centres = pltpu.make_async_copy(centres_hbm, centres, local_sem.at[0])
    load_coef = pltpu.make_async_copy(coef_hbm, coef, local_sem.at[1])
    load_centres.start()
    load_coef.start()

    def chip(k):
        p = lax.rem(dev + k, n_dev)
        return p, {"grp": grp, "dev": p}

    def core(k):
        p = lax.rem(grp + k, n_grp)
        return p, {"grp": p, "dev": dev}

    barrier = pltpu.get_barrier_semaphore()

    @pl.loop(1, n_dev)
    def _(k):
        pl.semaphore_signal(barrier, inc=1, device_id=chip(k)[1], device_id_type=MESH)

    for k in range(1, n_grp):
        pl.semaphore_signal(barrier, inc=1, device_id=core(k)[1], device_id_type=MESH)

    def block(ref, p, size):
        return ref.at[pl.ds(pl.multiple_of(p * size, size), size)]

    def chip_copy(ref, size, slot, k):
        mine = block(ref, me, size)
        return pltpu.make_async_remote_copy(
            src_ref=mine, dst_ref=mine, send_sem=send_sem.at[slot], recv_sem=recv_sem.at[slot, k],
            device_id=chip(k)[1], device_id_type=MESH)

    def pass_on(ref, size, slot, source):
        piece = block(ref, grp * n_dev + source, size)
        for k in range(1, n_grp):
            pltpu.make_async_remote_copy(
                src_ref=piece, dst_ref=piece, send_sem=pass_send.at[slot], recv_sem=pass_recv.at[slot],
                device_id=core(k)[1], device_id_type=MESH).start()

    def gather_start(ref, size, slot):
        @pl.loop(1, n_dev)
        def _(k):
            chip_copy(ref, size, slot, k).start()

        pass_on(ref, size, slot, dev)

    def gather_pass(ref, size, slot):
        @pl.loop(1, n_dev)
        def _(k):
            chip_copy(ref, size, slot, k).wait_recv()
            pass_on(ref, size, slot, lax.rem(dev + n_dev - k, n_dev))

    def many(ref, count, send, recv, where):
        piece = ref.at[pl.ds(0, count)]
        return pltpu.make_async_remote_copy(
            src_ref=piece, dst_ref=piece, send_sem=send, recv_sem=recv, device_id=where, device_id_type=MESH)

    def passed(ref, size, slot):
        return many(ref, (n_grp - 1) * n_dev * size, pass_send.at[slot], pass_recv.at[slot], core(1)[1])

    def gather_sent(ref, size, slot):
        many(ref, (n_dev - 1) * size, send_sem.at[slot], recv_sem.at[slot, 0], chip(1)[1]).wait_send()
        passed(ref, size, slot).wait_send()

    pick = one_hot(bidx, nidx, c_dev, 0)
    block(eigs, me, s_dev)[...] = eig[...]
    pl.semaphore_wait(barrier, (n_dev - 1) + (n_grp - 1))
    gather_start(eigs, s_dev, 2)

    load_centres.wait()
    own = mm(pick, centres[...]).astype(jnp.bfloat16)
    block(rows, me, b_dev)[...] = own[:b_dev]
    block(nys, me, s_dev)[...] = own[b_dev:]
    gather_start(rows, b_dev, 0)

    step = 256 if c_dev % 256 == 0 else 128

    @pl.loop(0, c_dev // step)
    def _(i):
        piece = pl.ds(pl.multiple_of(i * step, step), step)
        csq[piece, :] = square_column(centres[piece, :])

    load_coef.wait()
    coef_bf[...] = coef[...].astype(jnp.bfloat16)
    target[...] = jnp.zeros_like(target)
    target[:, 0:outs] = targets[...]
    acc[...] = jnp.zeros_like(acc)

    width = acc.shape[1]
    gather_pass(rows, b_dev, 0)
    gather_start(nys, s_dev, 1)

    per_band = band // width

    @pl.loop(0, n_grp * per_band)
    def _(j):
        @pl.when(j == per_band)
        def _():
            passed(rows, b_dev, 0).wait_recv()

        first = lax.rem(grp + j // per_band, n_grp) * band + lax.rem(j, per_band) * width
        across = pl.ds(pl.multiple_of(first, width), width)
        piece_rows = rows[across, :]
        bsq = square_row(piece_rows)
        minus_two = piece_rows * jnp.bfloat16(-2.0)
        sums = jnp.zeros((outs, width), jnp.float32)
        for i in range(c_dev // step):
            down = slice(i * step, (i + 1) * step)
            k = laplace(centres[down, :], csq[down, :], minus_two, bsq, rate).astype(jnp.bfloat16)
            sums = sums + mm(coef_bf[:, down], k)
        acc[0:outs, :] = sums
        part[across, :] = jnp.transpose(acc[...])

    for k in range(1, n_grp):
        g, where = core(k)
        pltpu.make_async_remote_copy(
            src_ref=block(part, g, band), dst_ref=pair.at[pl.ds((k - 1) * band, band)],
            send_sem=pair_send, recv_sem=pair_recv, device_id=where, device_id_type=MESH).start()
    pairs = many(pair, (n_grp - 1) * band, pair_send, pair_recv, core(1)[1])
    pairs.wait_recv()
    both = block(part, grp, band)[...]
    for k in range(1, n_grp):
        both = both + pair[(k - 1) * band:k * band, :]
    summed[...] = both

    @pl.loop(1, n_dev)
    def _(k):
        p, where = chip(k)
        pltpu.make_async_remote_copy(
            src_ref=block(summed, p, b_dev), dst_ref=block(got, dev, b_dev),
            send_sem=sum_send, recv_sem=sum_recv, device_id=where, device_id_type=MESH).start()

    block(got, dev, b_dev)[...] = block(summed, dev, b_dev)[...]

    gather_pass(eigs, s_dev, 2)
    gather_pass(nys, s_dev, 1)
    sums_in = many(got, (n_dev - 1) * b_dev, sum_send, sum_recv, chip(1)[1])

    def make_gain():
        passed(eigs, s_dev, 2).wait_recv()
        passed(nys, s_dev, 1).wait_recv()
        weights = mm(eig[...] * scale[...], eigs[...], NT, HIGHEST)
        tall = min(512, sub)
        span = min(512, batch)

        @pl.loop(0, batch // span)
        def _(j):
            across = pl.ds(pl.multiple_of(j * span, span), span)
            piece_rows = rows[across, :]
            bsq = square_row(piece_rows)
            minus_two = piece_rows * jnp.bfloat16(-2.0)
            total_gain = jnp.zeros((s_dev, span), jnp.float32)
            for i in range(sub // tall):
                piece_nys = nys[i * tall:(i + 1) * tall, :]
                kn = laplace(piece_nys, square_column(piece_nys), minus_two, bsq, rate)
                total_gain = total_gain + mm(weights[:, i * tall:(i + 1) * tall], kn, NN, HIGHEST)
            gain[:, across] = total_gain

    sums_in.wait_recv()
    own_res = jnp.sum(got[...].reshape(n_dev, b_dev, wide_out), axis=0) - target[...]
    block(res, me, b_dev)[...] = own_res
    gather_start(res, b_dev, 3)
    change[0:b_dev, :] = own_res
    make_gain()
    gather_pass(res, b_dev, 3)
    passed(res, b_dev, 3).wait_recv()
    change[b_dev:, :] = mm(gain[...], res[...], NN, HIGHEST)

    for slot, ref, size in ((0, rows, b_dev), (1, nys, s_dev), (2, eigs, s_dev), (3, res, b_dev)):
        gather_sent(ref, size, slot)
    pairs.wait_send()
    sums_in.wait_send()


def update_kernel(bidx, nidx, change, coef, updated, res_out):
    outs, width = coef.shape
    b_dev = bidx.shape[0]
    pick = one_hot(bidx, nidx, width, pl.program_id(0) * width)
    own_res = change[0:b_dev, :]
    both = jnp.concatenate([-own_res, change[b_dev:, :]], axis=0)
    high = both.astype(jnp.bfloat16)
    rest = both - high.astype(jnp.float32)
    middle = rest.astype(jnp.bfloat16)
    low = (rest - middle.astype(jnp.float32)).astype(jnp.bfloat16)
    both3 = jnp.concatenate([high, middle, low], axis=0)
    pick3 = jnp.concatenate([pick] * 3, axis=0)
    updated[...] = coef[...] + mm(both3, pick3, TN)[0:outs]
    res_out[...] = own_res[:, 0:outs]


def per_device(n_grp, n_dev, centres, coefficients, targets, batch_index, nys_index, eigvecs, eig_scale):
    n = n_grp * n_dev
    c_dev, feat = centres.shape
    outs = coefficients.shape[0]
    b_dev, s_dev, q = batch_index.shape[0], nys_index.shape[0], eigvecs.shape[1]
    batch, sub, band = n * b_dev, n * s_dev, n_dev * b_dev
    wide_out = -(-outs // 128) * 128
    width = min(512, band)
    vmem = pl.BlockSpec(memory_space=pltpu.VMEM)
    smem = pl.BlockSpec(memory_space=pltpu.SMEM)
    hbm = pl.BlockSpec(memory_space=pl.ANY)
    f32, bf16, dma = jnp.float32, jnp.bfloat16, pltpu.SemaphoreType.DMA
    change = pl.pallas_call(
        functools.partial(kernel, n_grp, n_dev),
        out_shape=jax.ShapeDtypeStruct((b_dev + s_dev, wide_out), f32),
        in_specs=[smem, smem, vmem, vmem, vmem, hbm, hbm],
        out_specs=vmem,
        scratch_shapes=[
            pltpu.VMEM((c_dev, feat), bf16),
            pltpu.VMEM((outs, c_dev), f32),
            pltpu.VMEM((outs, c_dev), bf16),
            pltpu.VMEM((c_dev, 128), f32),
            pltpu.VMEM((batch, feat), bf16),
            pltpu.VMEM((sub, feat), bf16),
            pltpu.VMEM((sub, q), f32),
            pltpu.VMEM((wide_out, width), f32),
            pltpu.VMEM((batch, wide_out), f32),
            pltpu.VMEM(((n_grp - 1) * band, wide_out), f32),
            pltpu.VMEM((band, wide_out), f32),
            pltpu.VMEM((band, wide_out), f32),
            pltpu.VMEM((batch, wide_out), f32),
            pltpu.VMEM((s_dev, batch), f32),
            pltpu.VMEM((b_dev, wide_out), f32),
            dma((2,)), dma((4,)), dma((4, n_dev)), dma((4,)), dma((4,)), dma, dma, dma, dma,
        ],
        compiler_params=pltpu.CompilerParams(
            collective_id=0, has_side_effects=True, vmem_limit_bytes=56 * 1024 * 1024),
    )(batch_index, nys_index, eig_scale.reshape(1, q), targets.T, eigvecs, centres, coefficients)
    columns = 1024 if c_dev % 1024 == 0 else c_dev
    whole = pl.BlockSpec((b_dev + s_dev, wide_out), lambda i: (0, 0))
    tile = pl.BlockSpec((outs, columns), lambda i: (0, i))
    updated, residual = pl.pallas_call(
        update_kernel,
        grid=(c_dev // columns,),
        out_shape=(jax.ShapeDtypeStruct((outs, c_dev), f32), jax.ShapeDtypeStruct((b_dev, outs), f32)),
        in_specs=[smem, smem, whole, tile],
        out_specs=(tile, pl.BlockSpec((b_dev, outs), lambda i: (0, 0))),
    )(batch_index, nys_index, change, coefficients)
    return updated, residual.T


def solution(mesh):
    both = ("grp", "dev")
    in_specs = (P(both, None), P(None, both), P(None, both), P(both), P(both), P(both, None), P())
    out_specs = (P(None, both), P(None, both))
    return jax.shard_map(
        functools.partial(per_device, mesh.shape["grp"], mesh.shape["dev"]),
        mesh=mesh, in_specs=in_specs, out_specs=out_specs, check_vma=False)
```

```python
import functools
import math

import jax
import jax.numpy as jnp
from jax import lax
from jax.experimental import pallas as pl
from jax.experimental.pallas import tpu as pltpu
from jax.sharding import PartitionSpec as P

MESH = pl.DeviceIdType.MESH
HIGHEST = lax.Precision.HIGHEST
NN = (((1,), (0,)), ((), ()))
NT = (((1,), (1,)), ((), ()))
TN = (((0,), (0,)), ((), ()))


def mm(a, b, dims=NN, precision=None):
    return lax.dot_general(a, b, dims, precision=precision, preferred_element_type=jnp.float32)


def split_square(x):
    f = x.astype(jnp.float32)
    f = f * f
    high = f.astype(jnp.bfloat16)
    low = (f - high.astype(jnp.float32)).astype(jnp.bfloat16)
    return high, low


def square_column(x):
    high, low = split_square(x)
    ones = jnp.ones((x.shape[1], 128), jnp.bfloat16)
    return mm(high, ones) + mm(low, ones)


def square_row(x):
    high, low = split_square(x)
    ones = jnp.ones((8, x.shape[1]), jnp.bfloat16)
    return (mm(ones, high, NT) + mm(ones, low, NT))[0:1]


def laplace(left, left_sq, minus_two_right, right_sq, rate):
    cross = mm(left, minus_two_right, NT)
    wide = jnp.concatenate([left_sq] * (cross.shape[1] // 128), axis=1)
    d2 = jnp.maximum((wide + right_sq) + cross, 1.0)
    return jnp.exp2((d2 * lax.rsqrt(d2)) * rate)


def one_hot(bidx, nidx, c_dev, first):
    b_dev, s_dev = bidx.shape[0], nidx.shape[0]
    total = b_dev + s_dev
    spot = lax.broadcasted_iota(jnp.int32, (total, 128), 0)
    index = jnp.zeros((total, 128), jnp.int32)
    for r in range(b_dev):
        index = jnp.where(spot == r, bidx[r], index)
    for r in range(s_dev):
        index = jnp.where(spot == b_dev + r, nidx[r], index)
    index = jnp.concatenate([index - first] * (c_dev // 128), axis=1)
    hit = lax.broadcasted_iota(jnp.int32, (total, c_dev), 1) == index
    return jnp.where(hit, 1.0, 0.0).astype(jnp.bfloat16)


def kernel(n_grp, n_dev, bidx, nidx, scale, targets, eig, centres_hbm, coef_hbm,
           change,
           centres, coef, coef_bf, csq, rows, nys, eigs, acc, part, pair, summed, got, res, gain, target,
           local_sem, send_sem, recv_sem, pass_send, pass_recv, pair_send, pair_recv, sum_send, sum_recv):
    n = n_grp * n_dev
    grp, dev = lax.axis_index("grp"), lax.axis_index("dev")
    me = grp * n_dev + dev
    c_dev, feat = centres.shape
    outs = coef.shape[0]
    b_dev, s_dev = bidx.shape[0], nidx.shape[0]
    batch, sub = rows.shape[0], nys.shape[0]
    rate = -1.0 / (0.7 * math.sqrt(feat) * math.log(2.0))
    wide_out = part.shape[1]
    band = n_dev * b_dev

    load_centres = pltpu.make_async_copy(centres_hbm, centres, local_sem.at[0])
    load_coef = pltpu.make_async_copy(coef_hbm, coef, local_sem.at[1])
    load_centres.start()
    load_coef.start()

    def chip(k):
        p = lax.rem(dev + k, n_dev)
        return p, {"grp": grp, "dev": p}

    def core(k):
        p = lax.rem(grp + k, n_grp)
        return p, {"grp": p, "dev": dev}

    barrier = pltpu.get_barrier_semaphore()

    @pl.loop(1, n_dev)
    def _(k):
        pl.semaphore_signal(barrier, inc=1, device_id=chip(k)[1], device_id_type=MESH)

    for k in range(1, n_grp):
        pl.semaphore_signal(barrier, inc=1, device_id=core(k)[1], device_id_type=MESH)

    def block(ref, p, size):
        return ref.at[pl.ds(pl.multiple_of(p * size, size), size)]

    def chip_copy(ref, size, slot, k):
        mine = block(ref, me, size)
        return pltpu.make_async_remote_copy(
            src_ref=mine, dst_ref=mine, send_sem=send_sem.at[slot], recv_sem=recv_sem.at[slot, k],
            device_id=chip(k)[1], device_id_type=MESH)

    def pass_on(ref, size, slot, source):
        piece = block(ref, grp * n_dev + source, size)
        for k in range(1, n_grp):
            pltpu.make_async_remote_copy(
                src_ref=piece, dst_ref=piece, send_sem=pass_send.at[slot], recv_sem=pass_recv.at[slot],
                device_id=core(k)[1], device_id_type=MESH).start()

    def gather_start(ref, size, slot):
        @pl.loop(1, n_dev)
        def _(k):
            chip_copy(ref, size, slot, k).start()

        pass_on(ref, size, slot, dev)

    def gather_pass(ref, size, slot):
        @pl.loop(1, n_dev)
        def _(k):
            chip_copy(ref, size, slot, k).wait_recv()
            pass_on(ref, size, slot, lax.rem(dev + n_dev - k, n_dev))

    def many(ref, count, send, recv, where):
        piece = ref.at[pl.ds(0, count)]
        return pltpu.make_async_remote_copy(
            src_ref=piece, dst_ref=piece, send_sem=send, recv_sem=recv, device_id=where, device_id_type=MESH)

    def passed(ref, size, slot):
        return many(ref, (n_grp - 1) * n_dev * size, pass_send.at[slot], pass_recv.at[slot], core(1)[1])

    def gather_sent(ref, size, slot):
        many(ref, (n_dev - 1) * size, send_sem.at[slot], recv_sem.at[slot, 0], chip(1)[1]).wait_send()
        passed(ref, size, slot).wait_send()

    pick = one_hot(bidx, nidx, c_dev, 0)
    block(eigs, me, s_dev)[...] = eig[...]
    pl.semaphore_wait(barrier, (n_dev - 1) + (n_grp - 1))
    gather_start(eigs, s_dev, 2)

    load_centres.wait()
    own = mm(pick, centres[...]).astype(jnp.bfloat16)
    block(rows, me, b_dev)[...] = own[:b_dev]
    block(nys, me, s_dev)[...] = own[b_dev:]
    gather_start(rows, b_dev, 0)

    step = 256 if c_dev % 256 == 0 else 128

    @pl.loop(0, c_dev // step)
    def _(i):
        piece = pl.ds(pl.multiple_of(i * step, step), step)
        csq[piece, :] = square_column(centres[piece, :])

    load_coef.wait()
    coef_bf[...] = coef[...].astype(jnp.bfloat16)
    target[...] = jnp.zeros_like(target)
    target[:, 0:outs] = targets[...]
    acc[...] = jnp.zeros_like(acc)

    width = acc.shape[1]
    gather_pass(rows, b_dev, 0)
    gather_start(nys, s_dev, 1)

    per_band = band // width

    @pl.loop(0, n_grp * per_band)
    def _(j):
        @pl.when(j == per_band)
        def _():
            passed(rows, b_dev, 0).wait_recv()

        first = lax.rem(grp + j // per_band, n_grp) * band + lax.rem(j, per_band) * width
        across = pl.ds(pl.multiple_of(first, width), width)
        piece_rows = rows[across, :]
        bsq = square_row(piece_rows)
        minus_two = piece_rows * jnp.bfloat16(-2.0)
        sums = jnp.zeros((outs, width), jnp.float32)
        for i in range(c_dev // step):
            down = slice(i * step, (i + 1) * step)
            k = laplace(centres[down, :], csq[down, :], minus_two, bsq, rate).astype(jnp.bfloat16)
            sums = sums + mm(coef_bf[:, down], k)
        acc[0:outs, :] = sums
        part[across, :] = jnp.transpose(acc[...])

    for k in range(1, n_grp):
        g, where = core(k)
        pltpu.make_async_remote_copy(
            src_ref=block(part, g, band), dst_ref=pair.at[pl.ds((k - 1) * band, band)],
            send_sem=pair_send, recv_sem=pair_recv, device_id=where, device_id_type=MESH).start()
    pairs = many(pair, (n_grp - 1) * band, pair_send, pair_recv, core(1)[1])
    pairs.wait_recv()
    both = block(part, grp, band)[...]
    for k in range(1, n_grp):
        both = both + pair[(k - 1) * band:k * band, :]
    summed[...] = both

    @pl.loop(1, n_dev)
    def _(k):
        p, where = chip(k)
        pltpu.make_async_remote_copy(
            src_ref=block(summed, p, b_dev), dst_ref=block(got, dev, b_dev),
            send_sem=sum_send, recv_sem=sum_recv, device_id=where, device_id_type=MESH).start()

    block(got, dev, b_dev)[...] = block(summed, dev, b_dev)[...]

    sums_in = many(got, (n_dev - 1) * b_dev, sum_send, sum_recv, chip(1)[1])

    def make_gain():
        passed(eigs, s_dev, 2).wait_recv()
        passed(nys, s_dev, 1).wait_recv()
        weights = mm(eig[...] * scale[...], eigs[...], NT, HIGHEST)
        tall = min(512, sub)
        span = min(512, batch)

        @pl.loop(0, batch // span)
        def _(j):
            across = pl.ds(pl.multiple_of(j * span, span), span)
            piece_rows = rows[across, :]
            bsq = square_row(piece_rows)
            minus_two = piece_rows * jnp.bfloat16(-2.0)
            total_gain = jnp.zeros((s_dev, span), jnp.float32)
            for i in range(sub // tall):
                piece_nys = nys[i * tall:(i + 1) * tall, :]
                kn = laplace(piece_nys, square_column(piece_nys), minus_two, bsq, rate)
                total_gain = total_gain + mm(weights[:, i * tall:(i + 1) * tall], kn, NN, HIGHEST)
            gain[:, across] = total_gain

    sums_in.wait_recv()
    own_res = jnp.sum(got[...].reshape(n_dev, b_dev, wide_out), axis=0) - target[...]
    block(res, me, b_dev)[...] = own_res
    gather_start(res, b_dev, 3)
    change[0:b_dev, :] = own_res
    gather_pass(eigs, s_dev, 2)
    gather_pass(nys, s_dev, 1)
    make_gain()
    gather_pass(res, b_dev, 3)
    passed(res, b_dev, 3).wait_recv()
    change[b_dev:, :] = mm(gain[...], res[...], NN, HIGHEST)

    for slot, ref, size in ((0, rows, b_dev), (1, nys, s_dev), (2, eigs, s_dev), (3, res, b_dev)):
        gather_sent(ref, size, slot)
    pairs.wait_send()
    sums_in.wait_send()


def update_kernel(bidx, nidx, change, coef, updated, res_out):
    outs, width = coef.shape
    b_dev = bidx.shape[0]
    pick = one_hot(bidx, nidx, width, pl.program_id(0) * width)
    own_res = change[0:b_dev, :]
    both = jnp.concatenate([-own_res, change[b_dev:, :]], axis=0)
    high = both.astype(jnp.bfloat16)
    rest = both - high.astype(jnp.float32)
    middle = rest.astype(jnp.bfloat16)
    low = (rest - middle.astype(jnp.float32)).astype(jnp.bfloat16)
    both3 = jnp.concatenate([high, middle, low], axis=0)
    pick3 = jnp.concatenate([pick] * 3, axis=0)
    updated[...] = coef[...] + mm(both3, pick3, TN)[0:outs]
    res_out[...] = own_res[:, 0:outs]


def per_device(n_grp, n_dev, centres, coefficients, targets, batch_index, nys_index, eigvecs, eig_scale):
    n = n_grp * n_dev
    c_dev, feat = centres.shape
    outs = coefficients.shape[0]
    b_dev, s_dev, q = batch_index.shape[0], nys_index.shape[0], eigvecs.shape[1]
    batch, sub, band = n * b_dev, n * s_dev, n_dev * b_dev
    wide_out = -(-outs // 128) * 128
    width = min(512, band)
    vmem = pl.BlockSpec(memory_space=pltpu.VMEM)
    smem = pl.BlockSpec(memory_space=pltpu.SMEM)
    hbm = pl.BlockSpec(memory_space=pl.ANY)
    f32, bf16, dma = jnp.float32, jnp.bfloat16, pltpu.SemaphoreType.DMA
    change = pl.pallas_call(
        functools.partial(kernel, n_grp, n_dev),
        out_shape=jax.ShapeDtypeStruct((b_dev + s_dev, wide_out), f32),
        in_specs=[smem, smem, vmem, vmem, vmem, hbm, hbm],
        out_specs=vmem,
        scratch_shapes=[
            pltpu.VMEM((c_dev, feat), bf16),
            pltpu.VMEM((outs, c_dev), f32),
            pltpu.VMEM((outs, c_dev), bf16),
            pltpu.VMEM((c_dev, 128), f32),
            pltpu.VMEM((batch, feat), bf16),
            pltpu.VMEM((sub, feat), bf16),
            pltpu.VMEM((sub, q), f32),
            pltpu.VMEM((wide_out, width), f32),
            pltpu.VMEM((batch, wide_out), f32),
            pltpu.VMEM(((n_grp - 1) * band, wide_out), f32),
            pltpu.VMEM((band, wide_out), f32),
            pltpu.VMEM((band, wide_out), f32),
            pltpu.VMEM((batch, wide_out), f32),
            pltpu.VMEM((s_dev, batch), f32),
            pltpu.VMEM((b_dev, wide_out), f32),
            dma((2,)), dma((4,)), dma((4, n_dev)), dma((4,)), dma((4,)), dma, dma, dma, dma,
        ],
        compiler_params=pltpu.CompilerParams(
            collective_id=0, has_side_effects=True, vmem_limit_bytes=56 * 1024 * 1024),
    )(batch_index, nys_index, eig_scale.reshape(1, q), targets.T, eigvecs, centres, coefficients)
    columns = 1024 if c_dev % 1024 == 0 else c_dev
    whole = pl.BlockSpec((b_dev + s_dev, wide_out), lambda i: (0, 0))
    tile = pl.BlockSpec((outs, columns), lambda i: (0, i))
    updated, residual = pl.pallas_call(
        update_kernel,
        grid=(c_dev // columns,),
        out_shape=(jax.ShapeDtypeStruct((outs, c_dev), f32), jax.ShapeDtypeStruct((b_dev, outs), f32)),
        in_specs=[smem, smem, whole, tile],
        out_specs=(tile, pl.BlockSpec((b_dev, outs), lambda i: (0, 0))),
    )(batch_index, nys_index, change, coefficients)
    return updated, residual.T


def solution(mesh):
    both = ("grp", "dev")
    in_specs = (P(both, None), P(None, both), P(None, both), P(both), P(both), P(both, None), P())
    out_specs = (P(None, both), P(None, both))
    return jax.shard_map(
        functools.partial(per_device, mesh.shape["grp"], mesh.shape["dev"]),
        mesh=mesh, in_specs=in_specs, out_specs=out_specs, check_vma=False)
```
